256 devices in a mesh: wide: 16 (over y, z_lo), narrow: 16 (over x, z_hi, core).
Axes of the slice: x: 4, y: 4, z: 8 (z_hi: 2, z_lo: 4; z = z_hi * 4 + z_lo), core: 2. Of those that a mesh axis runs over, the one named last changes fastest.
Arguments:
- residual: float32 [16, 16, 6, 192, 512], P('wide', 'narrow'), may hold values from -6 to 6
- face_schur: float32 [16, 16, 6, 192, 192], P('wide', 'narrow'), may hold values from -0.5 to 1.5, as said below
- local_solver: bfloat16 [16, 16, 1152, 1152], P('wide', 'narrow'), may hold values from -0.1875 to 0.1875
- interface_functional_set: float32 [3, 192, 16], replicated, may hold values from -0.4375 to 0.4375
- coarse_inverse: float32 [12288, 12288], P('wide', 'narrow'), may hold values from -0.109375 to 0.109375
Outputs:
- preconditioned: float32 [16, 16, 3, 192, 512], P('wide', 'narrow')
The draws below stay inside these ranges and needn't reach their ends.
Inputs may be any that keep to these rules, and one draw needn't show every extreme that they name: `face_schur`: every face block is symmetric positive definite.
All inputs are finite; a program needn't handle non-finite values. Where the reference program divides by a largest or mean magnitude, that divisor is 1e-20 or more.
Results may differ from the reference program's by a relative error of at most 0.002.
Values sent between devices are 32-bit elements; how exact they have to be, the bound alone decides.
A program may use at most 64 MiB of HBM per device.

```python
import jax
import jax.numpy as jnp
from jax import lax

F = 192
CF = 16
R = 512
NS_STEPS = 12
LOC = 1152
SUB_ROWS = 16
SUB_COLS = 16
NC = 12288


def draw_face_schur(key, part):
    scale_key, random_seed_blend = jax.random.split(jax.random.fold_in(key, 17))
    leading = (SUB_ROWS, SUB_COLS, 6)
    lowest = jnp.log(0.05)
    mixing = jax.random.normal(random_seed_blend, leading + (F, F), jnp.float32)
    stiffness = jnp.exp(jax.random.uniform(scale_key, leading + (F,), jnp.float32, 0.0, 1.0) * (0.0 - lowest) + lowest)
    mixing = (mixing + jnp.swapaxes(mixing, -1, -2)) * (0.2 / jnp.sqrt(2.0 * F))
    rooted = jnp.sqrt(stiffness)
    identity = jnp.eye(F, dtype=jnp.float32)
    return rooted[..., :, None] * (identity + mixing) * rooted[..., None, :]


def steps_of(own_key, extent, shards, least, top_value):
    factor_of, own = 1.0, jax.random.fold_in(own_key, 6)
    for position, parts in shards:
        steps = jnp.exp(jax.random.uniform(jax.random.fold_in(own, position), (parts,), jnp.float32, least / len(shards), top_value / len(shards)))
        factor_of = factor_of * jnp.repeat(steps, extent[position] // parts).reshape([-1 if axis == position else 1 for axis in range(len(extent))])
    return factor_of


def noise(own_key, dims, scale, bound, cuts=(), held_as=jnp.bfloat16):
    level = steps_of(own_key, dims, cuts, -0.22, 0.18) if cuts else 1.0
    drawn = jax.random.normal(own_key, dims, jnp.float32) * scale * level
    return jnp.minimum(jnp.maximum(drawn, -bound), bound).astype(held_as)


def setup_inputs(seed: int = 0) -> dict:
    keys = jax.random.split(jax.random.key(seed), 6)
    return {
        "residual": noise(keys[0], (SUB_ROWS, SUB_COLS, 6, F, R), 1.0, 6.0, ((0, 16), (1, 16)), jnp.float32),
        "face_schur": draw_face_schur(jax.random.fold_in(keys[5], 71), 0),
        "local_solver": noise(keys[2], (SUB_ROWS, SUB_COLS, LOC, LOC), LOC ** -0.5, 0.1875, ((0, 16), (1, 16))),
        "interface_functional_set": noise(keys[3], (3, F, CF), F ** -0.5, 0.4375, (), jnp.float32),
        "coarse_inverse": noise(keys[4], (NC, NC), (NC // 4) ** -0.5, 0.109375, ((0, 16), (1, 16)), jnp.float32),
    }


exact_arithmetic_mode = lax.Precision.HIGHEST


def newton_schulz(matrices):
    row_sums = jnp.max(jnp.sum(jnp.abs(matrices), axis=2), axis=1)
    approx = matrices / (row_sums * row_sums)[:, None, None]
    for iteration in range(NS_STEPS):
        product = jnp.einsum("bij,bjk->bik", matrices, approx, precision=exact_arithmetic_mode)
        approx = 2.0 * approx - jnp.einsum("bij,bjk->bik", approx, product, precision=exact_arithmetic_mode)
    return approx


def reference(residual, face_schur, local_solver, interface_functional_set, coarse_inverse):
    rows_count = residual.shape[0]
    cols_count = residual.shape[1]
    upper_wide = face_schur[:, :, 1] + jnp.roll(face_schur[:, :, 0], -1, axis=0)
    upper_narrow = face_schur[:, :, 3] + jnp.roll(face_schur[:, :, 2], -1, axis=1)
    vertical = face_schur[:, :, 4] + face_schur[:, :, 5]
    face_sums = jnp.stack([upper_wide, upper_narrow, vertical], axis=2)
    inverse = newton_schulz(face_sums.reshape(-1, F, F)).reshape(face_sums.shape)
    load_wide = residual[:, :, 1] + jnp.roll(residual[:, :, 0], -1, axis=0)
    load_narrow = residual[:, :, 3] + jnp.roll(residual[:, :, 2], -1, axis=1)
    load_vertical = residual[:, :, 4] + residual[:, :, 5]
    assembled_vector = jnp.stack([load_wide, load_narrow, load_vertical], axis=2)
    scaled = jnp.einsum("wngij,wngjr->wngir", inverse, assembled_vector, precision=exact_arithmetic_mode)
    face_scaled = jnp.stack([jnp.roll(scaled[:, :, 0], 1, axis=0), scaled[:, :, 0],
                             jnp.roll(scaled[:, :, 1], 1, axis=1), scaled[:, :, 1],
                             scaled[:, :, 2], scaled[:, :, 2]], axis=2)
    local_loads = jnp.einsum("wnfij,wnfjr->wnfir", face_schur, face_scaled, precision=exact_arithmetic_mode).astype(jnp.bfloat16)
    flattened = local_loads.reshape(-1, LOC, R)
    solvers = local_solver.reshape(-1, LOC, LOC)

    def solve_one(pair):
        return jnp.dot(pair[0], pair[1], preferred_element_type=jnp.float32)

    solved = lax.map(solve_one, (solvers, flattened)).reshape(rows_count, cols_count, 6, F, R)
    weighted = jnp.einsum("wnfij,wnfjr->wnfir", face_schur, solved, precision=exact_arithmetic_mode)
    combined = jnp.stack([weighted[:, :, 1] + jnp.roll(weighted[:, :, 0], -1, axis=0),
                          weighted[:, :, 3] + jnp.roll(weighted[:, :, 2], -1, axis=1),
                          weighted[:, :, 4] + weighted[:, :, 5]], axis=2)
    local_part = jnp.einsum("wngij,wngjr->wngir", inverse, combined, precision=exact_arithmetic_mode)
    restricted_residual = jnp.einsum("ehd,maeht->maedt", interface_functional_set, assembled_vector, precision=exact_arithmetic_mode)
    column_order = jnp.transpose(restricted_residual, (1, 0, 2, 3, 4)).reshape(NC, R)
    coarse_space = jnp.dot(coarse_inverse, column_order, precision=exact_arithmetic_mode, preferred_element_type=jnp.float32)
    coarse_space = coarse_space.reshape(rows_count, cols_count, 3, CF, R)
    coarse_component = jnp.einsum("luo,vqlos->vqlus", interface_functional_set, coarse_space, precision=exact_arithmetic_mode)
    return local_part + coarse_component
```

```python
import jax
import jax.numpy as jnp
from jax import lax
from jax.experimental import pallas as pl
from jax.experimental.pallas import tpu as pltpu
from jax.sharding import PartitionSpec as P

NS_STEPS = 12
F = 192
FP = 256
R = 512
CB = 48
HALF = 256
MESH = pl.DeviceIdType.MESH
F32 = jnp.float32
BF16 = jnp.bfloat16


def split(x):
    high = x.astype(BF16)
    return high, (x - high.astype(F32)).astype(BF16)


def mul(a, b):
    return jnp.dot(a, b, preferred_element_type=F32)


def mul3(ah, al, bh, bl):
    return mul(ah, bh) + (mul(ah, bl) + mul(al, bh))


def exact(a, b):
    return jnp.dot(a, b, precision=lax.Precision.HIGHEST, preferred_element_type=F32)


def kernel(
    r_hbm, s_hbm, l_hbm, phi_ref, c_hbm, o_hbm,
    rv, sv, lv, cv, rr, sr, small, small_in, gath,
    part, q1, q2, q3, coarse,
    mh, ml, x, xh, xl, ph, plo, sh, sl,
    bh, bl, loads, wsend, wrecv, comb, ov,
    loc, ss, rs,
):
    w = lax.axis_index("wide")
    n = lax.axis_index("narrow")
    y, zl = w // 4, w % 4
    xx, zh, c = n // 4, (n // 2) % 2, n % 2
    w_up, w_dn = (w + 1) % 16, (w + 15) % 16
    n_up, n_dn = (n + 1) % 16, (n + 15) % 16
    z_peers = [(y * 4 + (zl + d) % 4, n) for d in (1, 2, 3)]
    y_peers = [(((y + d) % 4) * 4 + zl, n) for d in (1, 2, 3)]
    x_peers = [(w, ((xx + d) % 4) * 4 + zh * 2 + c) for d in (1, 2, 3)]
    core_peer = (w, n + 1 - 2 * c)
    far_peer = (w, xx * 4 + (1 - zh) * 2 + c)

    local = [
        pltpu.make_async_copy(s_hbm.at[0, 0], sv, loc.at[0]),
        pltpu.make_async_copy(r_hbm.at[0, 0], rv, loc.at[1]),
        pltpu.make_async_copy(c_hbm, cv, loc.at[2]),
        pltpu.make_async_copy(l_hbm.at[0, 0], lv, loc.at[3]),
    ]
    for copy in local:
        copy.start()

    barrier = pltpu.get_barrier_semaphore()
    greeted = [(w_up, n), (w_dn, n), (w, n_up), (w, n_dn)]
    greeted += z_peers + y_peers + x_peers + [core_peer, far_peer]
    for peer in greeted:
        pl.semaphore_signal(barrier, inc=1, device_id=peer, device_id_type=MESH)
    pl.semaphore_wait(barrier, len(greeted))

    sent = []

    def send(src, dst, peer):
        i = len(sent)
        copy = pltpu.make_async_remote_copy(
            src_ref=src, dst_ref=dst, send_sem=ss.at[i], recv_sem=rs.at[i],
            device_id=peer, device_id_type=MESH,
        )
        copy.start()
        sent.append(copy)
        return copy

    faces_to = {2: (3, (w, n_dn)), 3: (2, (w, n_up)), 0: (1, (w_dn, n)), 1: (0, (w_up, n))}

    s_in = {}
    for f in (2, 3, 0, 1):
        slot, peer = faces_to[f]
        s_in[slot] = send(s_hbm.at[0, 0, f], sr.at[slot], peer)

    phit = [phi_ref[g].T for g in range(3)]
    local[1].wait()
    small[0] = exact(phit[1], rv[2])
    narrow_piece = send(small.at[0], small_in.at[0], (w, n_dn))
    small[1] = exact(phit[0], rv[0])
    wide_piece = send(small.at[1], small_in.at[1], (w_dn, n))
    own0 = exact(phit[0], rv[1])
    own1 = exact(phit[1], rv[3])
    own2 = exact(phit[2], rv[4] + rv[5])
    narrow_piece.wait_recv()
    wide_piece.wait_recv()
    gath[w, 0:16] = own0 + small_in[1]
    gath[w, 16:32] = own1 + small_in[0]
    gath[w, 32:48] = own2
    z_in = [send(gath.at[w], gath.at[w], peer) for peer in z_peers]
    y_in = [send(gath.at[w], gath.at[w], peer) for peer in y_peers]

    r_in = {}
    for f in (2, 3, 0, 1):
        slot, peer = faces_to[f]
        for k in range(2):
            cols = pl.ds(k * HALF, HALF)
            r_in[slot, k] = send(r_hbm.at[0, 0, f, :, cols], rr.at[slot, :, cols], peer)

    local[0].wait()
    sh[...] = jnp.zeros_like(sh)
    sl[...] = jnp.zeros_like(sl)
    mh[...] = jnp.zeros_like(mh)
    ml[...] = jnp.zeros_like(ml)
    x[...] = jnp.zeros_like(x)
    xh[...] = jnp.zeros_like(xh)
    xl[...] = jnp.zeros_like(xl)
    ph[:, F:FP] = jnp.zeros((5, FP - F, FP), BF16)
    plo[:, F:FP] = jnp.zeros((5, FP - F, FP), BF16)
    bh[:, F:FP] = jnp.zeros((6, FP - F, R), BF16)
    bl[:, F:FP] = jnp.zeros((6, FP - F, R), BF16)
    for f in range(6):
        high, low = split(sv[f])
        sh[f, :, 0:F] = high
        sl[f, :, 0:F] = low

    for f in (4, 2, 3, 0, 1):
        if f == 4:
            total = sv[4] + sv[5]
        else:
            s_in[f].wait_recv()
            total = sv[f] + sr[f]
        high, low = split(total)
        mh[f, :, 0:F] = high
        ml[f, :, 0:F] = low
        largest = jnp.max(jnp.sum(jnp.abs(total), axis=1, keepdims=True), axis=0, keepdims=True)
        start = total / (largest * largest)
        x[f, :, 0:F] = start
        high, low = split(start)
        xh[f, 0:F, 0:F] = high
        xl[f, 0:F, 0:F] = low

    def newton(step, carry):
        for f in range(5):
            high, low = split(mul3(mh[f], ml[f], xh[f], xl[f]))
            ph[f, 0:F] = high
            plo[f, 0:F] = low
        for f in range(5):
            new = 2.0 * x[f] - mul3(xh[f, 0:F], xl[f, 0:F], ph[f], plo[f])
            x[f] = new
            high, low = split(new)
            xh[f, 0:F] = high
            xl[f, 0:F] = low
        return carry

    lax.fori_loop(0, 4, newton, 0)
    for copy, d in zip(z_in, (1, 2, 3)):
        copy.wait_recv()
        block = gath.at[y * 4 + (zl + 4 - d) % 4]
        y_in += [send(block, block, peer) for peer in y_peers]
    lax.fori_loop(4, NS_STEPS, newton, 0)

    local[2].wait()
    for copy in y_in:
        copy.wait_recv()
    ch, cl = split(cv[...])
    for k in range(2):
        cols = slice(k * HALF, (k + 1) * HALF)
        gh, gl = split(gath[:, :, cols].reshape(768, HALF))
        value = mul3(ch, cl, gh, gl)
        for j in range(16):
            part[j % 2, j // 2, :, cols] = value[j * CB:(j + 1) * CB]
    pair_in = send(part.at[1 - c], q1, core_peer)
    pair_in.wait_recv()
    for b in range(8):
        part[c, b] = part[c, b] + q1[b]
    x_in = []
    for d in (1, 2, 3):
        first = ((xx + d) % 4) * 2
        x_in.append(send(part.at[c, pl.ds(first, 2)], q2.at[d - 1], x_peers[d - 1]))
    for copy in x_in:
        copy.wait_recv()
    for h in range(2):
        part[c, xx * 2 + h] = part[c, xx * 2 + h] + (q2[0, h] + (q2[1, h] + q2[2, h]))
    far_in = send(part.at[c, xx * 2 + 1 - zh], q3, far_peer)
    far_in.wait_recv()
    coarse[...] = part[c, xx * 2 + zh] + q3[...]

    local[3].wait()
    w_in = {}
    for k in range(2):
        cols = slice(k * HALF, (k + 1) * HALF)
        dcols = pl.ds(k * HALF, HALF)
        for f in (4, 2, 3, 0, 1):
            if f == 4:
                value = rv[4, :, cols] + rv[5, :, cols]
            else:
                r_in[f, k].wait_recv()
                value = rv[f, :, cols] + rr[f, :, cols]
            ah, al = split(value)
            bh[f, 0:F, cols] = ah
            bl[f, 0:F, cols] = al
        for f in range(5):
            high, low = split(mul3(xh[f, 0:F], xl[f, 0:F], bh[f, :, cols], bl[f, :, cols]))
            bh[f, 0:F, cols] = high
            bl[f, 0:F, cols] = low
        for f in range(6):
            s = min(f, 4)
            loads[f * F:(f + 1) * F, cols] = mul3(sh[f], sl[f], bh[s, :, cols], bl[s, :, cols]).astype(BF16)
        for f in (2, 0, 3, 1, 4, 5):
            high, low = split(mul(lv[f * F:(f + 1) * F, :], loads[:, cols]))
            bh[f, 0:F, cols] = high
            bl[f, 0:F, cols] = low
            value = mul3(sh[f], sl[f], bh[f, :, cols], bl[f, :, cols])
            if f == 2:
                wsend[1, :, cols] = value
                w_in[1, k] = send(wsend.at[1, :, dcols], wrecv.at[1, :, dcols], (w, n_dn))
            elif f == 0:
                wsend[0, :, cols] = value
                w_in[0, k] = send(wsend.at[0, :, dcols], wrecv.at[0, :, dcols], (w_dn, n))
            elif f == 5:
                comb[2, :, cols] = comb[2, :, cols] + value
            else:
                comb[f // 2, :, cols] = value

    out = []
    for g in (2, 1, 0):
        low_phi = phi_ref[g]
        for k in range(2):
            cols = slice(k * HALF, (k + 1) * HALF)
            value = comb[g, :, cols]
            if g < 2:
                w_in[g, k].wait_recv()
                value = value + wrecv[g, :, cols]
            high, low = split(value)
            bh[g, 0:F, cols] = high
            bl[g, 0:F, cols] = low
            f = (1, 3, 4)[g]
            ov[g, :, cols] = mul3(
                xh[f, 0:F], xl[f, 0:F], bh[g, :, cols], bl[g, :, cols]
            ) + exact(low_phi, coarse[g * 16:(g + 1) * 16, cols])
        copy = pltpu.make_async_copy(ov.at[g], o_hbm.at[0, 0, g], loc.at[4 + g])
        copy.start()
        out.append(copy)
    for copy in out:
        copy.wait()
    for copy in sent:
        copy.wait_send()


def per_device(residual, face_schur, local_solver, interface_functional_set, coarse_inverse):
    anywhere = pl.BlockSpec(memory_space=pl.ANY)
    vmem = pltpu.VMEM
    return pl.pallas_call(
        kernel,
        out_shape=jax.ShapeDtypeStruct((1, 1, 3, F, R), F32),
        in_specs=[anywhere, anywhere, anywhere, pl.BlockSpec(memory_space=vmem), anywhere],
        out_specs=anywhere,
        scratch_shapes=[
            vmem((6, F, R), F32), vmem((6, F, F), F32), vmem((1152, 1152), BF16), vmem((768, 768), F32),
            vmem((4, F, R), F32), vmem((4, F, F), F32), vmem((2, 16, R), F32), vmem((2, 16, R), F32),
            vmem((16, CB, R), F32),
            vmem((2, 8, CB, R), F32), vmem((8, CB, R), F32), vmem((3, 2, CB, R), F32), vmem((CB, R), F32),
            vmem((CB, R), F32),
            vmem((5, F, FP), BF16), vmem((5, F, FP), BF16), vmem((5, F, FP), F32),
            vmem((5, FP, FP), BF16), vmem((5, FP, FP), BF16), vmem((5, FP, FP), BF16), vmem((5, FP, FP), BF16),
            vmem((6, F, FP), BF16), vmem((6, F, FP), BF16),
            vmem((6, FP, R), BF16), vmem((6, FP, R), BF16), vmem((1152, R), BF16),
            vmem((2, F, R), F32), vmem((2, F, R), F32), vmem((3, F, R), F32), vmem((3, F, R), F32),
            pltpu.SemaphoreType.DMA((7,)), pltpu.SemaphoreType.DMA((48,)), pltpu.SemaphoreType.DMA((48,)),
        ],
        compiler_params=pltpu.CompilerParams(
            collective_id=0, has_side_effects=True, vmem_limit_bytes=56 * 1024 * 1024
        ),
    )(residual, face_schur, local_solver, interface_functional_set, coarse_inverse)


def solution(mesh):
    placed = (
        P("wide", "narrow", None, None, None),
        P("wide", "narrow", None, None, None),
        P("wide", "narrow", None, None),
        P(),
        P("wide", "narrow"),
    )
    return jax.shard_map(
        per_device,
        mesh=mesh,
        in_specs=placed,
        out_specs=P("wide", "narrow", None, None, None),
        check_vma=False,
    )
```

```python
import jax
import jax.numpy as jnp
from jax import lax
from jax.experimental import pallas as pl
from jax.experimental.pallas import tpu as pltpu
from jax.sharding import PartitionSpec as P

NS_STEPS = 12
F = 192
FP = 256
R = 512
CB = 48
HALF = 256
CHUNKS = ((0, 128), (128, 128), (256, 128), (384, 128))
EARLY = ("n0", "w0")
DURING = ((0, "n1"), (0, "w1"), (3, "fw"), (4, "n2"), (4, "w2"), (7, "n3"), (7, "w3"))
AFTER = ("l0", "cp", "l1", "cf", "l2", "l3", "ce")
MESH = pl.DeviceIdType.MESH
F32 = jnp.float32
BF16 = jnp.bfloat16


def split(x):
    high = x.astype(BF16)
    return high, (x - high.astype(F32)).astype(BF16)


def mul(a, b):
    return jnp.dot(a, b, preferred_element_type=F32)


def mul3(ah, al, bh, bl):
    return mul(ah, bh) + (mul(ah, bl) + mul(al, bh))


def exact(a, b):
    return jnp.dot(a, b, precision=lax.Precision.HIGHEST, preferred_element_type=F32)


def kernel(
    r_hbm, s_hbm, l_hbm, phi_ref, c_hbm, o_hbm,
    rv, sv, lv, cv, rr, sr, spk, spk_in, small, small_in, gath,
    part, q1, q2, q3, coarse,
    mh, ml, x, xh, xl, ph, plo, sh, sl,
    bh, bl, loads, wsend, wrecv, comb, ov,
    loc, ss, rs,
):
    w = lax.axis_index("wide")
    n = lax.axis_index("narrow")
    y, zl = w // 4, w % 4
    xx, zh, c = n // 4, (n // 2) % 2, n % 2
    w_up, w_dn = (w + 1) % 16, (w + 15) % 16
    n_up, n_dn = (n + 1) % 16, (n + 15) % 16
    z_peers = [(y * 4 + (zl + d) % 4, n) for d in (1, 2, 3)]
    y_peers = [(((y + d) % 4) * 4 + zl, n) for d in (1, 2, 3)]
    x_peers = [(w, ((xx + d) % 4) * 4 + zh * 2 + c) for d in (1, 2, 3)]
    core_peer = (w, n + 1 - 2 * c)
    far_peer = (w, xx * 4 + (1 - zh) * 2 + c)

    local = [
        pltpu.make_async_copy(s_hbm.at[0, 0], sv, loc.at[0]),
        pltpu.make_async_copy(r_hbm.at[0, 0], rv, loc.at[1]),
        pltpu.make_async_copy(c_hbm, cv, loc.at[2]),
        pltpu.make_async_copy(l_hbm.at[0, 0], lv, loc.at[3]),
    ]
    local[0].start()
    local[1].start()

    barrier = pltpu.get_barrier_semaphore()
    greeted = [(w_up, n), (w_dn, n), (w, n_up), (w, n_dn)]
    greeted += z_peers + y_peers + x_peers + [core_peer, far_peer]
    for peer in greeted:
        pl.semaphore_signal(barrier, inc=1, device_id=peer, device_id_type=MESH)

    left = lax.broadcasted_iota(jnp.int32, (64, 128), 1) < 64
    local[0].wait()
    for f in range(4):
        top, middle, bottom = (sv[f, 64 * i:64 * i + 64, 0:128] for i in range(3))
        spk[f, 0:64] = jnp.where(left, top, middle)
        spk[f, 64:128] = bottom
        spk[f, 64:128, 0:64] = sv[f, 128:192, 128:192]
        spk[f, 128:192] = jnp.where(left, bottom, top)
    pl.semaphore_wait(barrier, len(greeted))

    sent = []

    def send(src, dst, peer):
        i = len(sent)
        copy = pltpu.make_async_remote_copy(
            src_ref=src, dst_ref=dst, send_sem=ss.at[i], recv_sem=rs.at[i],
            device_id=peer, device_id_type=MESH,
        )
        copy.start()
        sent.append(copy)
        return copy

    faces_to = {2: (3, (w, n_dn)), 3: (2, (w, n_up)), 0: (1, (w_dn, n)), 1: (0, (w_up, n))}

    s_in = {}
    for f in (2, 3, 0, 1):
        slot, peer = faces_to[f]
        s_in[slot] = send(spk.at[f], spk_in.at[slot], peer)
    local[2].start()
    local[3].start()

    phit = [phi_ref[g].T for g in range(3)]
    local[1].wait()
    small[0] = exact(phit[1], rv[2])
    narrow_piece = send(small.at[0], small_in.at[0], (w, n_dn))
    small[1] = exact(phit[0], rv[0])
    wide_piece = send(small.at[1], small_in.at[1], (w_dn, n))
    own0 = exact(phit[0], rv[1])
    own1 = exact(phit[1], rv[3])
    own2 = exact(phit[2], rv[4] + rv[5])
    narrow_piece.wait_recv()
    wide_piece.wait_recv()
    gath[w, 0:16] = own0 + small_in[1]
    gath[w, 16:32] = own1 + small_in[0]
    gath[w, 32:48] = own2
    z_in = [send(gath.at[w], gath.at[w], peer) for peer in z_peers]
    y_in = [send(gath.at[w], gath.at[w], peer) for peer in y_peers]

    r_in = {}

    def send_loads(faces, k):
        cols = pl.ds(*CHUNKS[k])
        for f in faces:
            slot, peer = faces_to[f]
            r_in[slot, k] = send(r_hbm.at[0, 0, f, :, cols], rr.at[slot, :, cols], peer)

    def forward():
        for copy, d in zip(z_in, (1, 2, 3)):
            copy.wait_recv()
            block = gath.at[y * 4 + (zl + 4 - d) % 4]
            for peer in y_peers:
                y_in.append(send(block, block, peer))

    actions = {"fw": forward}
    for k in range(len(CHUNKS)):
        actions[f"n{k}"] = lambda k=k: send_loads((2, 3), k)
        actions[f"w{k}"] = lambda k=k: send_loads((0, 1), k)
    for name in EARLY:
        actions[name]()

    sh[...] = jnp.zeros_like(sh)
    sl[...] = jnp.zeros_like(sl)
    mh[...] = jnp.zeros_like(mh)
    ml[...] = jnp.zeros_like(ml)
    x[...] = jnp.zeros_like(x)
    xh[...] = jnp.zeros_like(xh)
    xl[...] = jnp.zeros_like(xl)
    ph[:, F:FP] = jnp.zeros((5, FP - F, FP), BF16)
    plo[:, F:FP] = jnp.zeros((5, FP - F, FP), BF16)
    bh[:, F:FP] = jnp.zeros((6, FP - F, R), BF16)
    bl[:, F:FP] = jnp.zeros((6, FP - F, R), BF16)
    for f in range(6):
        high, low = split(sv[f])
        sh[f, :, 0:F] = high
        sl[f, :, 0:F] = low

    for f in (4, 2, 3, 0, 1):
        if f == 4:
            total = sv[4] + sv[5]
        else:
            s_in[f].wait_recv()
            first, second, third = (spk_in[f, 64 * i:64 * i + 64] for i in range(3))
            second_t, third_t = second.T, third.T
            sr[f, 0:64, 0:128] = jnp.where(left, first, third)
            sr[f, 64:128, 0:128] = first
            sr[f, 64:128, 0:64] = third_t[64:128]
            sr[f, 128:192, 0:128] = jnp.where(left, third, second)
            sr[f, 0:64, 128:192] = third_t[0:64]
            sr[f, 64:128, 128:192] = second_t[64:128]
            sr[f, 128:192, 128:192] = second[:, 0:64]
            total = sv[f] + sr[f]
        high, low = split(total)
        mh[f, :, 0:F] = high
        ml[f, :, 0:F] = low
        largest = jnp.max(jnp.sum(jnp.abs(total), axis=1, keepdims=True), axis=0, keepdims=True)
        start = total / (largest * largest)
        x[f, :, 0:F] = start
        high, low = split(start)
        xh[f, 0:F, 0:F] = high
        xl[f, 0:F, 0:F] = low

    def newton(step, carry):
        for f in range(5):
            high, low = split(mul3(mh[f], ml[f], xh[f], xl[f]))
            ph[f, 0:F] = high
            plo[f, 0:F] = low
        for f in range(5):
            new = 2.0 * x[f] - mul3(xh[f, 0:F], xl[f, 0:F], ph[f], plo[f])
            x[f] = new
            high, low = split(new)
            xh[f, 0:F] = high
            xl[f, 0:F] = low
        return carry

    done = 0
    for step, name in DURING:
        if step > done:
            lax.fori_loop(done, step, newton, 0)
            done = step
        actions[name]()
    if done < NS_STEPS:
        lax.fori_loop(done, NS_STEPS, newton, 0)

    w_in = {}

    def local_part(k):
        begin, width = CHUNKS[k]
        cols = slice(begin, begin + width)
        dcols = pl.ds(begin, width)
        for f in (4, 2, 3, 0, 1):
            if f == 4:
                value = rv[4, :, cols] + rv[5, :, cols]
            else:
                r_in[f, k].wait_recv()
                value = rv[f, :, cols] + rr[f, :, cols]
            ah, al = split(value)
            bh[f, 0:F, cols] = ah
            bl[f, 0:F, cols] = al
            high, low = split(mul3(xh[f, 0:F], xl[f, 0:F], bh[f, :, cols], bl[f, :, cols]))
            bh[f, 0:F, cols] = high
            bl[f, 0:F, cols] = low
            for g in ((4, 5) if f == 4 else (f,)):
                loads[g * F:(g + 1) * F, cols] = mul3(
                    sh[g], sl[g], bh[f, :, cols], bl[f, :, cols]
                ).astype(BF16)
        for f in (2, 0, 3, 1, 4, 5):
            high, low = split(mul(lv[f * F:(f + 1) * F, :], loads[:, cols]))
            bh[f, 0:F, cols] = high
            bl[f, 0:F, cols] = low
            value = mul3(sh[f], sl[f], bh[f, :, cols], bl[f, :, cols])
            if f == 2:
                wsend[1, :, cols] = value
                w_in[1, k] = send(wsend.at[1, :, dcols], wrecv.at[1, :, dcols], (w, n_dn))
            elif f == 0:
                wsend[0, :, cols] = value
                w_in[0, k] = send(wsend.at[0, :, dcols], wrecv.at[0, :, dcols], (w_dn, n))
            elif f == 5:
                comb[2, :, cols] = comb[2, :, cols] + value
            else:
                comb[f // 2, :, cols] = value

    x_in = []

    def coarse_product():
        for copy in y_in:
            copy.wait_recv()
        ch, cl = split(cv[...])
        for k in range(2):
            cols = slice(k * HALF, (k + 1) * HALF)
            gh, gl = split(gath[:, :, cols].reshape(768, HALF))
            value = mul3(ch, cl, gh, gl)
            for j in range(16):
                part[j % 2, j // 2, :, cols] = value[j * CB:(j + 1) * CB]
        pair_in = send(part.at[1 - c], q1, core_peer)
        pair_in.wait_recv()
        for b in range(8):
            part[c, b] = part[c, b] + q1[b]
        for d in (1, 2, 3):
            first = ((xx + d) % 4) * 2
            x_in.append(send(part.at[c, pl.ds(first, 2)], q2.at[d - 1], x_peers[d - 1]))

    far = []

    def coarse_far():
        for copy in x_in:
            copy.wait_recv()
        for h in range(2):
            part[c, xx * 2 + h] = part[c, xx * 2 + h] + (q2[0, h] + (q2[1, h] + q2[2, h]))
        far.append(send(part.at[c, xx * 2 + 1 - zh], q3, far_peer))

    def coarse_end():
        far[0].wait_recv()
        coarse[...] = part[c, xx * 2 + zh] + q3[...]
        for g in range(3):
            ov[g] = exact(phi_ref[g], coarse[g * 16:(g + 1) * 16])

    out = []

    def finish(g, k):
        begin, width = CHUNKS[k]
        cols = slice(begin, begin + width)
        dcols = pl.ds(begin, width)
        value = comb[g, :, cols]
        if g < 2:
            w_in[g, k].wait_recv()
            value = value + wrecv[g, :, cols]
        high, low = split(value)
        bh[g, 0:F, cols] = high
        bl[g, 0:F, cols] = low
        f = (1, 3, 4)[g]
        ov[g, :, cols] = ov[g, :, cols] + mul3(
            xh[f, 0:F], xl[f, 0:F], bh[g, :, cols], bl[g, :, cols]
        )
        copy = pltpu.make_async_copy(
            ov.at[g, :, dcols], o_hbm.at[0, 0, g, :, dcols], loc.at[4 + len(out)]
        )
        copy.start()
        out.append(copy)

    local[2].wait()
    local[3].wait()
    steps = {"cp": coarse_product, "cf": coarse_far, "ce": coarse_end}
    for k in range(len(CHUNKS)):
        steps[f"l{k}"] = lambda k=k: local_part(k)
    for name in AFTER:
        steps[name]()

    for k in range(len(CHUNKS)):
        finish(2, k)
    for k in range(len(CHUNKS)):
        finish(1, k)
        finish(0, k)
    for copy in out:
        copy.wait()
    for copy in sent:
        copy.wait_send()


def per_device(residual, face_schur, local_solver, interface_functional_set, coarse_inverse):
    anywhere = pl.BlockSpec(memory_space=pl.ANY)
    vmem = pltpu.VMEM
    return pl.pallas_call(
        kernel,
        out_shape=jax.ShapeDtypeStruct((1, 1, 3, F, R), F32),
        in_specs=[anywhere, anywhere, anywhere, pl.BlockSpec(memory_space=vmem), anywhere],
        out_specs=anywhere,
        scratch_shapes=[
            vmem((6, F, R), F32), vmem((6, F, F), F32), vmem((1152, 1152), BF16), vmem((768, 768), F32),
            vmem((4, F, R), F32), vmem((4, F, F), F32), vmem((4, F, 128), F32), vmem((4, F, 128), F32), vmem((2, 16, R), F32), vmem((2, 16, R), F32),
            vmem((16, CB, R), F32),
            vmem((2, 8, CB, R), F32), vmem((8, CB, R), F32), vmem((3, 2, CB, R), F32), vmem((CB, R), F32),
            vmem((CB, R), F32),
            vmem((5, F, FP), BF16), vmem((5, F, FP), BF16), vmem((5, F, FP), F32),
            vmem((5, FP, FP), BF16), vmem((5, FP, FP), BF16), vmem((5, FP, FP), BF16), vmem((5, FP, FP), BF16),
            vmem((6, F, FP), BF16), vmem((6, F, FP), BF16),
            vmem((6, FP, R), BF16), vmem((6, FP, R), BF16), vmem((1152, R), BF16),
            vmem((2, F, R), F32), vmem((2, F, R), F32), vmem((3, F, R), F32), vmem((3, F, R), F32),
            pltpu.SemaphoreType.DMA((16,)), pltpu.SemaphoreType.DMA((64,)), pltpu.SemaphoreType.DMA((64,)),
        ],
        compiler_params=pltpu.CompilerParams(
            collective_id=0, has_side_effects=True, vmem_limit_bytes=56 * 1024 * 1024
        ),
    )(residual, face_schur, local_solver, interface_functional_set, coarse_inverse)


def solution(mesh):
    placed = (
        P("wide", "narrow", None, None, None),
        P("wide", "narrow", None, None, None),
        P("wide", "narrow", None, None),
        P(),
        P("wide", "narrow"),
    )
    return jax.shard_map(
        per_device,
        mesh=mesh,
        in_specs=placed,
        out_specs=P("wide", "narrow", None, None, None),
        check_vma=False,
    )
```

```python
import jax
import jax.numpy as jnp
from jax import lax
from jax.experimental import pallas as pl
from jax.experimental.pallas import tpu as pltpu
from jax.sharding import PartitionSpec as P

NS_STEPS = 12
F = 192
FP = 256
R = 512
CB = 48
HALF = 256
CHUNKS = ((0, 128), (128, 256), (384, 128))
EARLY = ("n0", "w0")
DURING = ((0, "n1"), (0, "w1"), (0, "n2"), (0, "w2"), (4, "fw"))
AFTER = ("s0", "s1", "s2", "l0", "cp", "cx", "l1", "cf", "l2", "ce")
MESH = pl.DeviceIdType.MESH
F32 = jnp.float32
BF16 = jnp.bfloat16


def split(x):
    high = x.astype(BF16)
    return high, (x - high.astype(F32)).astype(BF16)


def mul(a, b):
    return jnp.dot(a, b, preferred_element_type=F32)


def mul3(ah, al, bh, bl):
    return mul(ah, bh) + (mul(ah, bl) + mul(al, bh))


def thin(ah, al, b):
    bh, bl = split(b)
    both = mul(jnp.concatenate([ah, al], axis=0), bh)
    rows = ah.shape[0]
    return both[:rows] + (both[rows:] + mul(ah, bl))


def exact(a, b):
    return jnp.dot(a, b, precision=lax.Precision.HIGHEST, preferred_element_type=F32)


def kernel(
    r_hbm, s_hbm, l_hbm, phi_ref, c_hbm, o_hbm,
    rv, sv, lv, cv, rr, sr, spk, spk_in, small, small_in, gath,
    part, q1, q2, q3, coarse,
    mh, ml, x, xh, xl, ph, plo, sh, sl,
    bh, bl, loads, ssend, srecv, wsend, wrecv, comb, ov,
    loc, ss, rs,
):
    w = lax.axis_index("wide")
    n = lax.axis_index("narrow")
    y, zl = w // 4, w % 4
    xx, zh, c = n // 4, (n // 2) % 2, n % 2
    w_up, w_dn = (w + 1) % 16, (w + 15) % 16
    n_up, n_dn = (n + 1) % 16, (n + 15) % 16
    z_peers = [(y * 4 + (zl + d) % 4, n) for d in (1, 2, 3)]
    y_peers = [(((y + d) % 4) * 4 + zl, n) for d in (1, 2, 3)]
    x_peers = [(w, ((xx + d) % 4) * 4 + zh * 2 + c) for d in (1, 2, 3)]
    core_peer = (w, n + 1 - 2 * c)
    far_peer = (w, xx * 4 + (1 - zh) * 2 + c)

    local = [
        pltpu.make_async_copy(s_hbm.at[0, 0], sv, loc.at[0]),
        pltpu.make_async_copy(r_hbm.at[0, 0], rv, loc.at[1]),
        pltpu.make_async_copy(c_hbm, cv, loc.at[2]),
        pltpu.make_async_copy(l_hbm.at[0, 0], lv, loc.at[3]),
    ]
    local[0].start()
    local[1].start()

    barrier = pltpu.get_barrier_semaphore()
    greeted = [(w_up, n), (w_dn, n), (w, n_up), (w, n_dn)]
    greeted += z_peers + y_peers + x_peers + [core_peer, far_peer]
    for peer in greeted:
        pl.semaphore_signal(barrier, inc=1, device_id=peer, device_id_type=MESH)

    left = lax.broadcasted_iota(jnp.int32, (64, 128), 1) < 64
    local[0].wait()
    for g in range(2):
        top, middle, bottom = (sv[2 * g, 64 * i:64 * i + 64, 0:128] for i in range(3))
        spk[g, 0:64] = jnp.where(left, top, middle)
        spk[g, 64:128] = bottom
        spk[g, 64:128, 0:64] = sv[2 * g, 128:192, 128:192]
        spk[g, 128:192] = jnp.where(left, bottom, top)
    pl.semaphore_wait(barrier, len(greeted))

    sent = []

    def send(src, dst, peer):
        i = len(sent)
        copy = pltpu.make_async_remote_copy(
            src_ref=src, dst_ref=dst, send_sem=ss.at[i], recv_sem=rs.at[i],
            device_id=peer, device_id_type=MESH,
        )
        copy.start()
        sent.append(copy)
        return copy

    lower = ((w_dn, n), (w, n_dn))
    upper = ((w_up, n), (w, n_up))
    s_in = {g: send(spk.at[g], spk_in.at[g], lower[g]) for g in (1, 0)}
    local[2].start()
    local[3].start()

    phit = [split(phi_ref[g]) for g in range(3)]
    local[1].wait()
    small[0] = thin(*phit[1], rv[2])
    narrow_piece = send(small.at[0], small_in.at[0], (w, n_dn))
    small[1] = thin(*phit[0], rv[0])
    wide_piece = send(small.at[1], small_in.at[1], (w_dn, n))
    own0 = thin(*phit[0], rv[1])
    own1 = thin(*phit[1], rv[3])
    own2 = thin(*phit[2], rv[4] + rv[5])
    narrow_piece.wait_recv()
    wide_piece.wait_recv()
    gath[w, 0:16] = own0 + small_in[1]
    gath[w, 16:32] = own1 + small_in[0]
    gath[w, 32:48] = own2
    z_in = [send(gath.at[w], gath.at[w], peer) for peer in z_peers]
    y_in = [send(gath.at[w], gath.at[w], peer) for peer in y_peers]

    r_in = {}

    def send_loads(g, k):
        cols = pl.ds(*CHUNKS[k])
        r_in[g, k] = send(r_hbm.at[0, 0, 2 * g, :, cols], rr.at[g, :, cols], lower[g])

    def forward():
        for copy, d in zip(z_in, (1, 2, 3)):
            copy.wait_recv()
            block = gath.at[y * 4 + (zl + 4 - d) % 4]
            for peer in y_peers:
                y_in.append(send(block, block, peer))

    actions = {"fw": forward}
    for k in range(len(CHUNKS)):
        actions[f"n{k}"] = lambda k=k: send_loads(1, k)
        actions[f"w{k}"] = lambda k=k: send_loads(0, k)
    for name in EARLY:
        actions[name]()

    sh[...] = jnp.zeros_like(sh)
    sl[...] = jnp.zeros_like(sl)
    mh[...] = jnp.zeros_like(mh)
    ml[...] = jnp.zeros_like(ml)
    x[...] = jnp.zeros_like(x)
    xh[...] = jnp.zeros_like(xh)
    xl[...] = jnp.zeros_like(xl)
    ph[:, F:FP] = jnp.zeros((3, FP - F, FP), BF16)
    plo[:, F:FP] = jnp.zeros((3, FP - F, FP), BF16)
    bh[:, F:FP] = jnp.zeros((6, FP - F, R), BF16)
    bl[:, F:FP] = jnp.zeros((6, FP - F, R), BF16)
    for f in range(6):
        high, low = split(sv[f])
        sh[f, :, 0:F] = high
        sl[f, :, 0:F] = low

    for g in (2, 1, 0):
        if g == 2:
            total = sv[4] + sv[5]
        else:
            s_in[g].wait_recv()
            first, second, third = (spk_in[g, 64 * i:64 * i + 64] for i in range(3))
            second_t, third_t = second.T, third.T
            sr[g, 0:64, 0:128] = jnp.where(left, first, third)
            sr[g, 64:128, 0:128] = first
            sr[g, 64:128, 0:64] = third_t[64:128]
            sr[g, 128:192, 0:128] = jnp.where(left, third, second)
            sr[g, 0:64, 128:192] = third_t[0:64]
            sr[g, 64:128, 128:192] = second_t[64:128]
            sr[g, 128:192, 128:192] = second[:, 0:64]
            total = sv[2 * g + 1] + sr[g]
        high, low = split(total)
        mh[g, :, 0:F] = high
        ml[g, :, 0:F] = low
        largest = jnp.max(jnp.sum(jnp.abs(total), axis=1, keepdims=True), axis=0, keepdims=True)
        start = total / (largest * largest)
        x[g, :, 0:F] = start
        high, low = split(start)
        xh[g, 0:F, 0:F] = high
        xl[g, 0:F, 0:F] = low

    def newton(step, carry):
        for g in range(3):
            high, low = split(mul3(mh[g], ml[g], xh[g], xl[g]))
            ph[g, 0:F] = high
            plo[g, 0:F] = low
        for g in range(3):
            new = 2.0 * x[g] - mul3(xh[g, 0:F], xl[g, 0:F], ph[g], plo[g])
            x[g] = new
            high, low = split(new)
            xh[g, 0:F] = high
            xl[g, 0:F] = low
        return carry

    done = 0
    for step, name in DURING:
        if step > done:
            lax.fori_loop(done, step, newton, 0)
            done = step
        actions[name]()
    if done < NS_STEPS:
        lax.fori_loop(done, NS_STEPS, newton, 0)

    w_in = {}

    y_scaled = {}

    def face_loads(f, slot, cols):
        loads[f * F:(f + 1) * F, cols] = mul3(
            sh[f], sl[f], bh[slot, :, cols], bl[slot, :, cols]
        ).astype(BF16)

    def scaled_part(k):
        begin, width = CHUNKS[k]
        cols = slice(begin, begin + width)
        dcols = pl.ds(begin, width)
        for g in (1, 0, 2):
            if g == 2:
                value = rv[4, :, cols] + rv[5, :, cols]
            else:
                r_in[g, k].wait_recv()
                value = rv[2 * g + 1, :, cols] + rr[g, :, cols]
            f = (1, 3, 4)[g]
            high, low = split(value)
            bh[f, 0:F, cols] = high
            bl[f, 0:F, cols] = low
            value = mul3(xh[g, 0:F], xl[g, 0:F], bh[f, :, cols], bl[f, :, cols])
            if g < 2:
                ssend[g, :, cols] = value
                y_scaled[g, k] = send(ssend.at[g, :, dcols], srecv.at[g, :, dcols], upper[g])
            high, low = split(value)
            bh[f, 0:F, cols] = high
            bl[f, 0:F, cols] = low
        for f in (1, 3, 4, 5):
            face_loads(f, min(f, 4), cols)

    def local_part(k):
        begin, width = CHUNKS[k]
        cols = slice(begin, begin + width)
        dcols = pl.ds(begin, width)
        for g in (0, 1):
            y_scaled[g, k].wait_recv()
            high, low = split(srecv[g, :, cols])
            bh[2 * g, 0:F, cols] = high
            bl[2 * g, 0:F, cols] = low
            face_loads(2 * g, 2 * g, cols)
        for f in (2, 0, 3, 1, 4, 5):
            high, low = split(mul(lv[f * F:(f + 1) * F, :], loads[:, cols]))
            bh[f, 0:F, cols] = high
            bl[f, 0:F, cols] = low
            value = mul3(sh[f], sl[f], bh[f, :, cols], bl[f, :, cols])
            if f == 2:
                wsend[1, :, cols] = value
                w_in[1, k] = send(wsend.at[1, :, dcols], wrecv.at[1, :, dcols], (w, n_dn))
            elif f == 0:
                wsend[0, :, cols] = value
                w_in[0, k] = send(wsend.at[0, :, dcols], wrecv.at[0, :, dcols], (w_dn, n))
            elif f == 5:
                comb[2, :, cols] = comb[2, :, cols] + value
            else:
                comb[f // 2, :, cols] = value

    x_in = []
    pair_in = []

    def coarse_product():
        for copy in y_in:
            copy.wait_recv()
        ch, cl = split(cv[...])
        for k in range(2):
            cols = slice(k * HALF, (k + 1) * HALF)
            gh, gl = split(gath[:, :, cols].reshape(768, HALF))
            value = mul3(ch, cl, gh, gl)
            for j in range(16):
                part[j % 2, j // 2, :, cols] = value[j * CB:(j + 1) * CB]
            dcols = pl.ds(k * HALF, HALF)
            pair_in.append(send(part.at[1 - c, :, :, dcols], q1.at[:, :, dcols], core_peer))

    def coarse_pair():
        for k in range(2):
            cols = slice(k * HALF, (k + 1) * HALF)
            dcols = pl.ds(k * HALF, HALF)
            pair_in[k].wait_recv()
            for b in range(8):
                part[c, b, :, cols] = part[c, b, :, cols] + q1[b, :, cols]
            for d in (1, 2, 3):
                first = ((xx + d) % 4) * 2
                x_in.append(send(
                    part.at[c, pl.ds(first, 2), :, dcols], q2.at[d - 1, :, :, dcols], x_peers[d - 1]
                ))

    far = []

    def coarse_far():
        for k in range(2):
            cols = slice(k * HALF, (k + 1) * HALF)
            dcols = pl.ds(k * HALF, HALF)
            for copy in x_in[3 * k:3 * k + 3]:
                copy.wait_recv()
            for h in range(2):
                part[c, xx * 2 + h, :, cols] = part[c, xx * 2 + h, :, cols] + (
                    q2[0, h, :, cols] + (q2[1, h, :, cols] + q2[2, h, :, cols])
                )
            far.append(send(part.at[c, xx * 2 + 1 - zh, :, dcols], q3.at[:, dcols], far_peer))

    def coarse_end():
        for copy in far:
            copy.wait_recv()
        coarse[...] = part[c, xx * 2 + zh] + q3[...]
        for g in range(3):
            ov[g] = exact(phi_ref[g].T, coarse[g * 16:(g + 1) * 16])

    out = []

    def finish(g, k):
        begin, width = CHUNKS[k]
        cols = slice(begin, begin + width)
        dcols = pl.ds(begin, width)
        value = comb[g, :, cols]
        if g < 2:
            w_in[g, k].wait_recv()
            value = value + wrecv[g, :, cols]
        high, low = split(value)
        bh[g, 0:F, cols] = high
        bl[g, 0:F, cols] = low
        ov[g, :, cols] = ov[g, :, cols] + mul3(
            xh[g, 0:F], xl[g, 0:F], bh[g, :, cols], bl[g, :, cols]
        )
        copy = pltpu.make_async_copy(
            ov.at[g, :, dcols], o_hbm.at[0, 0, g, :, dcols], loc.at[4 + len(out)]
        )
        copy.start()
        out.append(copy)

    local[2].wait()
    local[3].wait()
    steps = {"cp": coarse_product, "cx": coarse_pair, "cf": coarse_far, "ce": coarse_end}
    for k in range(len(CHUNKS)):
        steps[f"s{k}"] = lambda k=k: scaled_part(k)
        steps[f"l{k}"] = lambda k=k: local_part(k)
    for name in AFTER:
        steps[name]()

    for k in range(len(CHUNKS)):
        finish(2, k)
    for k in range(len(CHUNKS)):
        finish(1, k)
        finish(0, k)
    for copy in out:
        copy.wait()
    for copy in sent:
        copy.wait_send()


def per_device(residual, face_schur, local_solver, interface_functional_set, coarse_inverse):
    anywhere = pl.BlockSpec(memory_space=pl.ANY)
    vmem = pltpu.VMEM
    return pl.pallas_call(
        kernel,
        out_shape=jax.ShapeDtypeStruct((1, 1, 3, F, R), F32),
        in_specs=[anywhere, anywhere, anywhere, pl.BlockSpec(memory_space=vmem), anywhere],
        out_specs=anywhere,
        scratch_shapes=[
            vmem((6, F, R), F32), vmem((6, F, F), F32), vmem((1152, 1152), BF16), vmem((768, 768), F32),
            vmem((2, F, R), F32), vmem((2, F, F), F32), vmem((2, F, 128), F32), vmem((2, F, 128), F32), vmem((2, 16, R), F32), vmem((2, 16, R), F32),
            vmem((16, CB, R), F32),
            vmem((2, 8, CB, R), F32), vmem((8, CB, R), F32), vmem((3, 2, CB, R), F32), vmem((CB, R), F32),
            vmem((CB, R), F32),
            vmem((3, F, FP), BF16), vmem((3, F, FP), BF16), vmem((3, F, FP), F32),
            vmem((3, FP, FP), BF16), vmem((3, FP, FP), BF16), vmem((3, FP, FP), BF16), vmem((3, FP, FP), BF16),
            vmem((6, F, FP), BF16), vmem((6, F, FP), BF16),
            vmem((6, FP, R), BF16), vmem((6, FP, R), BF16), vmem((1152, R), BF16),
            vmem((2, F, R), F32), vmem((2, F, R), F32), vmem((2, F, R), F32), vmem((2, F, R), F32), vmem((3, F, R), F32), vmem((3, F, R), F32),
            pltpu.SemaphoreType.DMA((16,)), pltpu.SemaphoreType.DMA((64,)), pltpu.SemaphoreType.DMA((64,)),
        ],
        compiler_params=pltpu.CompilerParams(
            collective_id=0, has_side_effects=True, vmem_limit_bytes=56 * 1024 * 1024
        ),
    )(residual, face_schur, local_solver, jnp.swapaxes(interface_functional_set, 1, 2), coarse_inverse)


def solution(mesh):
    placed = (
        P("wide", "narrow", None, None, None),
        P("wide", "narrow", None, None, None),
        P("wide", "narrow", None, None),
        P(),
        P("wide", "narrow"),
    )
    return jax.shard_map(
        per_device,
        mesh=mesh,
        in_specs=placed,
        out_specs=P("wide", "narrow", None, None, None),
        check_vma=False,
    )
```

```python
import jax
import jax.numpy as jnp
from jax import lax
from jax.experimental import pallas as pl
from jax.experimental.pallas import tpu as pltpu
from jax.sharding import PartitionSpec as P

NS_STEPS = 12
F = 192
FP = 256
R = 512
CB = 48
HALF = 256
CHUNKS = ((0, 128), (128, 256), (384, 128))
FIRST = ("n0", "w0")
EARLY = ("n1", "w1")
DURING = ((0, "n2"), (0, "w2"), (3, "f1"), (6, "f3"), (9, "f2"))
AFTER = ("s0", "s1", "s2", "l0", "cp", "cx", "l1", "cf", "l2", "ce")
MESH = pl.DeviceIdType.MESH
F32 = jnp.float32
BF16 = jnp.bfloat16


def split(x):
    high = x.astype(BF16)
    return high, (x - high.astype(F32)).astype(BF16)


def mul(a, b):
    return jnp.dot(a, b, preferred_element_type=F32)


def mul3(ah, al, bh, bl):
    return mul(ah, bh) + (mul(ah, bl) + mul(al, bh))


def thin(ah, al, b):
    bh, bl = split(b)
    both = mul(jnp.concatenate([ah, al], axis=0), bh)
    rows = ah.shape[0]
    return both[:rows] + (both[rows:] + mul(ah, bl))


def exact(a, b):
    return jnp.dot(a, b, precision=lax.Precision.HIGHEST, preferred_element_type=F32)


def kernel(
    r_hbm, s_hbm, l_hbm, phi_ref, c_hbm, o_hbm,
    rv, sv, lv, cv, rr, sr, spk, spk_in, small, small_in, gath,
    part, q1, q2, q3, coarse,
    mh, ml, x, xh, xl, ph, plo, sh, sl,
    bh, bl, loads, ssend, srecv, wsend, wrecv, comb, ov,
    loc, ss, rs,
):
    w = lax.axis_index("wide")
    n = lax.axis_index("narrow")
    y, zl = w // 4, w % 4
    xx, zh, c = n // 4, (n // 2) % 2, n % 2
    w_up, w_dn = (w + 1) % 16, (w + 15) % 16
    n_up, n_dn = (n + 1) % 16, (n + 15) % 16
    z_peers = [(y * 4 + (zl + d) % 4, n) for d in (1, 2, 3)]
    y_peers = [(((y + d) % 4) * 4 + zl, n) for d in (1, 2, 3)]
    x_peers = [(w, ((xx + d) % 4) * 4 + zh * 2 + c) for d in (1, 2, 3)]
    core_peer = (w, n + 1 - 2 * c)
    far_peer = (w, xx * 4 + (1 - zh) * 2 + c)

    local = [
        pltpu.make_async_copy(s_hbm.at[0, 0], sv, loc.at[0]),
        pltpu.make_async_copy(r_hbm.at[0, 0], rv, loc.at[1]),
        pltpu.make_async_copy(c_hbm, cv, loc.at[2]),
        pltpu.make_async_copy(l_hbm.at[0, 0], lv, loc.at[3]),
    ]
    local[0].start()
    local[1].start()

    barrier = pltpu.get_barrier_semaphore()
    greeted = [(w_up, n), (w_dn, n), (w, n_up), (w, n_dn)]
    greeted += z_peers + y_peers + x_peers + [core_peer, far_peer]
    for peer in greeted:
        pl.semaphore_signal(barrier, inc=1, device_id=peer, device_id_type=MESH)

    left = lax.broadcasted_iota(jnp.int32, (64, 128), 1) < 64
    local[0].wait()
    for g in range(2):
        top, middle, bottom = (sv[2 * g, 64 * i:64 * i + 64, 0:128] for i in range(3))
        spk[g, 0:64] = jnp.where(left, top, middle)
        spk[g, 64:128] = bottom
        spk[g, 64:128, 0:64] = sv[2 * g, 128:192, 128:192]
        spk[g, 128:192] = jnp.where(left, bottom, top)
    pl.semaphore_wait(barrier, len(greeted))

    sent = []

    def send(src, dst, peer):
        i = len(sent)
        copy = pltpu.make_async_remote_copy(
            src_ref=src, dst_ref=dst, send_sem=ss.at[i], recv_sem=rs.at[i],
            device_id=peer, device_id_type=MESH,
        )
        copy.start()
        sent.append(copy)
        return copy

    lower = ((w_dn, n), (w, n_dn))
    upper = ((w_up, n), (w, n_up))
    s_in = {g: send(spk.at[g], spk_in.at[g], lower[g]) for g in (1, 0)}
    r_in = {}

    def send_loads(g, k):
        cols = pl.ds(*CHUNKS[k])
        r_in[g, k] = send(r_hbm.at[0, 0, 2 * g, :, cols], rr.at[g, :, cols], lower[g])

    def forward(d):
        z_in[d - 1].wait_recv()
        block = gath.at[y * 4 + (zl + 4 - d) % 4]
        for peer in y_peers:
            y_in.append(send(block, block, peer))

    actions = {f"f{d}": lambda d=d: forward(d) for d in (1, 2, 3)}
    for k in range(len(CHUNKS)):
        actions[f"n{k}"] = lambda k=k: send_loads(1, k)
        actions[f"w{k}"] = lambda k=k: send_loads(0, k)
    for name in FIRST:
        actions[name]()
    local[2].start()
    local[3].start()

    phit = [split(phi_ref[g]) for g in range(3)]
    local[1].wait()
    small[0] = thin(*phit[1], rv[2])
    narrow_piece = send(small.at[0], small_in.at[0], (w, n_dn))
    small[1] = thin(*phit[0], rv[0])
    wide_piece = send(small.at[1], small_in.at[1], (w_dn, n))
    own0 = thin(*phit[0], rv[1])
    own1 = thin(*phit[1], rv[3])
    own2 = thin(*phit[2], rv[4] + rv[5])
    narrow_piece.wait_recv()
    wide_piece.wait_recv()
    gath[w, 0:16] = own0 + small_in[1]
    gath[w, 16:32] = own1 + small_in[0]
    gath[w, 32:48] = own2
    z_in = [send(gath.at[w], gath.at[w], peer) for peer in z_peers]
    y_in = [send(gath.at[w], gath.at[w], peer) for peer in y_peers]

    for name in EARLY:
        actions[name]()

    sh[...] = jnp.zeros_like(sh)
    sl[...] = jnp.zeros_like(sl)
    mh[...] = jnp.zeros_like(mh)
    ml[...] = jnp.zeros_like(ml)
    x[...] = jnp.zeros_like(x)
    xh[...] = jnp.zeros_like(xh)
    xl[...] = jnp.zeros_like(xl)
    ph[:, F:FP] = jnp.zeros((3, FP - F, FP), BF16)
    plo[:, F:FP] = jnp.zeros((3, FP - F, FP), BF16)
    bh[:, F:FP] = jnp.zeros((6, FP - F, R), BF16)
    bl[:, F:FP] = jnp.zeros((6, FP - F, R), BF16)
    for f in range(6):
        high, low = split(sv[f])
        sh[f, :, 0:F] = high
        sl[f, :, 0:F] = low

    for g in (2, 1, 0):
        if g == 2:
            total = sv[4] + sv[5]
        else:
            s_in[g].wait_recv()
            first, second, third = (spk_in[g, 64 * i:64 * i + 64] for i in range(3))
            second_t, third_t = second.T, third.T
            sr[g, 0:64, 0:128] = jnp.where(left, first, third)
            sr[g, 64:128, 0:128] = first
            sr[g, 64:128, 0:64] = third_t[64:128]
            sr[g, 128:192, 0:128] = jnp.where(left, third, second)
            sr[g, 0:64, 128:192] = third_t[0:64]
            sr[g, 64:128, 128:192] = second_t[64:128]
            sr[g, 128:192, 128:192] = second[:, 0:64]
            total = sv[2 * g + 1] + sr[g]
        high, low = split(total)
        mh[g, :, 0:F] = high
        ml[g, :, 0:F] = low
        largest = jnp.max(jnp.sum(jnp.abs(total), axis=1, keepdims=True), axis=0, keepdims=True)
        start = total / (largest * largest)
        x[g, :, 0:F] = start
        high, low = split(start)
        xh[g, 0:F, 0:F] = high
        xl[g, 0:F, 0:F] = low

    def newton(step, carry):
        for g in range(3):
            high, low = split(mul3(mh[g], ml[g], xh[g], xl[g]))
            ph[g, 0:F] = high
            plo[g, 0:F] = low
        for g in range(3):
            new = 2.0 * x[g] - mul3(xh[g, 0:F], xl[g, 0:F], ph[g], plo[g])
            x[g] = new
            high, low = split(new)
            xh[g, 0:F] = high
            xl[g, 0:F] = low
        return carry

    done = 0
    for step, name in DURING:
        if step > done:
            lax.fori_loop(done, step, newton, 0)
            done = step
        actions[name]()
    if done < NS_STEPS:
        lax.fori_loop(done, NS_STEPS, newton, 0)

    w_in = {}

    y_scaled = {}

    def face_loads(f, slot, cols):
        loads[f * F:(f + 1) * F, cols] = mul3(
            sh[f], sl[f], bh[slot, :, cols], bl[slot, :, cols]
        ).astype(BF16)

    def scaled_part(k):
        begin, width = CHUNKS[k]
        cols = slice(begin, begin + width)
        dcols = pl.ds(begin, width)
        for g in (1, 0, 2):
            if g == 2:
                value = rv[4, :, cols] + rv[5, :, cols]
            else:
                r_in[g, k].wait_recv()
                value = rv[2 * g + 1, :, cols] + rr[g, :, cols]
            f = (1, 3, 4)[g]
            high, low = split(value)
            bh[f, 0:F, cols] = high
            bl[f, 0:F, cols] = low
            value = mul3(xh[g, 0:F], xl[g, 0:F], bh[f, :, cols], bl[f, :, cols])
            if g < 2:
                ssend[g, :, cols] = value
                y_scaled[g, k] = send(ssend.at[g, :, dcols], srecv.at[g, :, dcols], upper[g])
            high, low = split(value)
            bh[f, 0:F, cols] = high
            bl[f, 0:F, cols] = low
        for f in (1, 3, 4, 5):
            face_loads(f, min(f, 4), cols)

    def local_part(k):
        begin, width = CHUNKS[k]
        cols = slice(begin, begin + width)
        dcols = pl.ds(begin, width)
        for g in (0, 1):
            y_scaled[g, k].wait_recv()
            high, low = split(srecv[g, :, cols])
            bh[2 * g, 0:F, cols] = high
            bl[2 * g, 0:F, cols] = low
            face_loads(2 * g, 2 * g, cols)
        for f in (2, 0, 3, 1, 4, 5):
            high, low = split(mul(lv[f * F:(f + 1) * F, :], loads[:, cols]))
            bh[f, 0:F, cols] = high
            bl[f, 0:F, cols] = low
            value = mul3(sh[f], sl[f], bh[f, :, cols], bl[f, :, cols])
            if f == 2:
                wsend[1, :, cols] = value
                w_in[1, k] = send(wsend.at[1, :, dcols], wrecv.at[1, :, dcols], (w, n_dn))
            elif f == 0:
                wsend[0, :, cols] = value
                w_in[0, k] = send(wsend.at[0, :, dcols], wrecv.at[0, :, dcols], (w_dn, n))
            elif f == 5:
                comb[2, :, cols] = comb[2, :, cols] + value
            else:
                comb[f // 2, :, cols] = value

    x_in = []
    pair_in = []

    def coarse_product():
        for copy in y_in:
            copy.wait_recv()
        ch, cl = split(cv[...])
        for k in range(2):
            cols = slice(k * HALF, (k + 1) * HALF)
            gh, gl = split(gath[:, :, cols].reshape(768, HALF))
            value = mul3(ch, cl, gh, gl)
            for j in range(16):
                part[j % 2, j // 2, :, cols] = value[j * CB:(j + 1) * CB]
            dcols = pl.ds(k * HALF, HALF)
            pair_in.append(send(part.at[1 - c, :, :, dcols], q1.at[:, :, dcols], core_peer))

    def coarse_pair():
        for k in range(2):
            cols = slice(k * HALF, (k + 1) * HALF)
            dcols = pl.ds(k * HALF, HALF)
            pair_in[k].wait_recv()
            for b in range(8):
                part[c, b, :, cols] = part[c, b, :, cols] + q1[b, :, cols]
            for d in (1, 2, 3):
                first = ((xx + d) % 4) * 2
                x_in.append(send(
                    part.at[c, pl.ds(first, 2), :, dcols], q2.at[d - 1, :, :, dcols], x_peers[d - 1]
                ))

    far = []

    def coarse_far():
        for k in range(2):
            cols = slice(k * HALF, (k + 1) * HALF)
            dcols = pl.ds(k * HALF, HALF)
            for copy in x_in[3 * k:3 * k + 3]:
                copy.wait_recv()
            for h in range(2):
                part[c, xx * 2 + h, :, cols] = part[c, xx * 2 + h, :, cols] + (
                    q2[0, h, :, cols] + (q2[1, h, :, cols] + q2[2, h, :, cols])
                )
            far.append(send(part.at[c, xx * 2 + 1 - zh, :, dcols], q3.at[:, dcols], far_peer))

    def coarse_end():
        for copy in far:
            copy.wait_recv()
        coarse[...] = part[c, xx * 2 + zh] + q3[...]
        for g in range(3):
            ov[g] = exact(phi_ref[g].T, coarse[g * 16:(g + 1) * 16])

    out = []

    def finish(g, k):
        begin, width = CHUNKS[k]
        cols = slice(begin, begin + width)
        dcols = pl.ds(begin, width)
        value = comb[g, :, cols]
        if g < 2:
            w_in[g, k].wait_recv()
            value = value + wrecv[g, :, cols]
        high, low = split(value)
        bh[g, 0:F, cols] = high
        bl[g, 0:F, cols] = low
        ov[g, :, cols] = ov[g, :, cols] + mul3(
            xh[g, 0:F], xl[g, 0:F], bh[g, :, cols], bl[g, :, cols]
        )
        copy = pltpu.make_async_copy(
            ov.at[g, :, dcols], o_hbm.at[0, 0, g, :, dcols], loc.at[4 + len(out)]
        )
        copy.start()
        out.append(copy)

    local[2].wait()
    local[3].wait()
    steps = {"cp": coarse_product, "cx": coarse_pair, "cf": coarse_far, "ce": coarse_end}
    for k in range(len(CHUNKS)):
        steps[f"s{k}"] = lambda k=k: scaled_part(k)
        steps[f"l{k}"] = lambda k=k: local_part(k)
    for name in AFTER:
        steps[name]()

    for k in range(len(CHUNKS)):
        finish(2, k)
    for k in range(len(CHUNKS)):
        finish(1, k)
        finish(0, k)
    for copy in out:
        copy.wait()
    for copy in sent:
        copy.wait_send()


def per_device(residual, face_schur, local_solver, interface_functional_set, coarse_inverse):
    anywhere = pl.BlockSpec(memory_space=pl.ANY)
    vmem = pltpu.VMEM
    return pl.pallas_call(
        kernel,
        out_shape=jax.ShapeDtypeStruct((1, 1, 3, F, R), F32),
        in_specs=[anywhere, anywhere, anywhere, pl.BlockSpec(memory_space=vmem), anywhere],
        out_specs=anywhere,
        scratch_shapes=[
            vmem((6, F, R), F32), vmem((6, F, F), F32), vmem((1152, 1152), BF16), vmem((768, 768), F32),
            vmem((2, F, R), F32), vmem((2, F, F), F32), vmem((2, F, 128), F32), vmem((2, F, 128), F32), vmem((2, 16, R), F32), vmem((2, 16, R), F32),
            vmem((16, CB, R), F32),
            vmem((2, 8, CB, R), F32), vmem((8, CB, R), F32), vmem((3, 2, CB, R), F32), vmem((CB, R), F32),
            vmem((CB, R), F32),
            vmem((3, F, FP), BF16), vmem((3, F, FP), BF16), vmem((3, F, FP), F32),
            vmem((3, FP, FP), BF16), vmem((3, FP, FP), BF16), vmem((3, FP, FP), BF16), vmem((3, FP, FP), BF16),
            vmem((6, F, FP), BF16), vmem((6, F, FP), BF16),
            vmem((6, FP, R), BF16), vmem((6, FP, R), BF16), vmem((1152, R), BF16),
            vmem((2, F, R), F32), vmem((2, F, R), F32), vmem((2, F, R), F32), vmem((2, F, R), F32), vmem((3, F, R), F32), vmem((3, F, R), F32),
            pltpu.SemaphoreType.DMA((16,)), pltpu.SemaphoreType.DMA((64,)), pltpu.SemaphoreType.DMA((64,)),
        ],
        compiler_params=pltpu.CompilerParams(
            collective_id=0, has_side_effects=True, vmem_limit_bytes=56 * 1024 * 1024
        ),
    )(residual, face_schur, local_solver, jnp.swapaxes(interface_functional_set, 1, 2), coarse_inverse)


def solution(mesh):
    placed = (
        P("wide", "narrow", None, None, None),
        P("wide", "narrow", None, None, None),
        P("wide", "narrow", None, None),
        P(),
        P("wide", "narrow"),
    )
    return jax.shard_map(
        per_device,
        mesh=mesh,
        in_specs=placed,
        out_specs=P("wide", "narrow", None, None, None),
        check_vma=False,
    )
```
